256 devices in a mesh: mic: 16 (over z, x_hi), tm: 16 (over y, x_lo, core).
Axes of the slice: x: 4 (x_hi: 2, x_lo: 2; x = x_hi * 2 + x_lo), y: 4, z: 8, core: 2. Of those that a mesh axis runs over, the one named last changes fastest.
Arguments:
- signal: bfloat16 [512, 32768], P('mic', 'tm'), may hold values from -6 to 6
- delay: int32 [128, 512, 1024], P('tm', 'mic'), may hold values from 0 to 56
- fraction: float32 [512, 1024], P('mic'), may hold values from 0 to 1
- weight: float32 [512, 1024], P('mic'), may hold values from -0.25 to 0.25
Outputs:
- beam: float32 [1024, 32768], P('mic', 'tm')
The draws below stay inside these ranges and needn't reach their ends.
Inputs may be any that keep to these rules, and one draw needn't show every extreme that they name: Each delay leaves room for the eight taps inside the span of 64 samples.
All inputs are finite; a program needn't handle non-finite values.
Results may differ from the reference program's by a relative error of at most 0.0029.
Values may be sent and summed in bfloat16 or wider, within the bound.
A program may use at most 320 MiB of HBM per device.

```python
import math
import jax
import jax.numpy as jnp
from jax import lax

M = 512
F = 1024
L = 64
SUB = 256
TALL = 32768
NBLK = 128


def set_ends(entries, key, smallest, largest):
    extent = entries.shape
    index_at = [jax.random.randint(jax.random.fold_in(key, axis), (), 0, extent[axis]) for axis in range(len(extent))]
    entries = entries.at[tuple(index_at)].set(smallest)
    longest = extent.index(max(extent))
    index_at[longest] = (index_at[longest] + 1) % extent[longest]
    return entries.at[tuple(index_at)].set(largest)


def block_levels(key, shape, pieces, smallest, top_value):
    factor_of = 1.0
    for dim, shards_of in pieces:
        steps = jax.random.uniform(jax.random.fold_in(jax.random.fold_in(key, 6), dim), (shards_of,), jnp.float32, smallest / len(pieces), top_value / len(pieces))
        factor_of = factor_of * jnp.repeat(jnp.exp(steps), shape[dim] // shards_of).reshape((-1,) + (1,) * (len(shape) - 1 - dim))
    return factor_of


def gaussian(stream_key, shape, deviation, bound, split=(), kind=jnp.bfloat16):
    values = deviation * jax.random.normal(stream_key, shape, jnp.float32)
    if split:
        values = values * block_levels(stream_key, shape, split, -0.22, 0.18)
    return jnp.clip(values, -bound, bound).astype(kind)


def setup_inputs(seed: int = 0) -> dict:
    keys = jax.random.split(jax.random.key(seed), 5)
    return {
        "signal": gaussian(keys[0], (M, TALL), 1.0, 6.0, ((0, 16), (1, 16))),
        "delay": set_ends(jax.random.randint(keys[1], (NBLK, M, F), 0, L - 7), jax.random.fold_in(keys[1], 1), 0, (L - 7) - 1).astype(jnp.int32),
        "fraction": jnp.clip(1.0 * jax.random.uniform(keys[2], (M, F), jnp.float32) ** block_levels(keys[2], (M, F), ((0, 16),), -0.2, 0.2), 0.0, 1.0),
        "weight": gaussian(keys[3], (M, F), M ** -0.5, 0.25, ((0, 16),), jnp.float32),
    }


def coefficients(delay_block, fraction, weight):
    offsets = jnp.arange(L, dtype=jnp.int32)[None, :, None]
    relative = offsets - delay_block[:, None, :]
    shifted = relative.astype(jnp.float32) - 3.0 - fraction[:, None, :]
    window = jnp.cos(math.pi * shifted / 8.0)
    taps = jnp.sinc(shifted) * window * window
    inside = (relative >= 0) & (relative < 8)
    coef = jnp.where(inside, taps * weight[:, None, :], jnp.float32(0.0)).astype(jnp.bfloat16)
    return coef.reshape(-1, coef.shape[2])


def reference(signal, delay, fraction, weight):
    mics = signal.shape[0]
    padded = jnp.concatenate([signal, jnp.zeros((mics, L), jnp.bfloat16)], axis=1)
    lanes = jnp.arange(L, dtype=jnp.int32)[:, None] + jnp.arange(SUB, dtype=jnp.int32)[None, :]

    def one_block(index):
        start = (index * SUB).astype(jnp.int32)
        piece = lax.dynamic_slice_in_dim(padded, start, SUB + L, 1)
        delayed = piece[:, lanes].reshape(mics * L, SUB)
        coef = coefficients(delay[index], fraction, weight)
        return jnp.dot(coef.T, delayed, preferred_element_type=jnp.float32)

    blocks = lax.map(one_block, jnp.arange(delay.shape[0], dtype=jnp.int32))
    return jnp.transpose(blocks, (1, 0, 2)).reshape(blocks.shape[1], -1)
```

```python
import math

import jax
import jax.numpy as jnp
from jax import lax
from jax.experimental import pallas as pl
from jax.experimental.pallas import tpu as pltpu
from jax.sharding import PartitionSpec as P

MESH = pl.DeviceIdType.MESH
BF, F32, I16 = jnp.bfloat16, jnp.float32, jnp.int16
MICS, FOCUS, HALF, NB, SUB, TIME = 32, 1024, 512, 8, 256, 2048
RING = 8
WIDE = TIME + 128


def series(y, terms):
    r = jnp.full_like(y, terms[-1])
    for c in terms[-2::-1]:
        r = r * y + c
    return r


SIN = [(-1) ** k * math.pi ** (2 * k + 1) / math.factorial(2 * k + 1) for k in range(7)]
COS = [(-1) ** k * math.pi ** (2 * k) / math.factorial(2 * k) for k in range(6)]


def eight_taps(frac, weight):
    low = jnp.minimum(frac, 1.0 - frac)
    scaled = series(low * low, SIN) * low * weight * (1.0 / math.pi)
    quarter = frac * 0.25
    square = quarter * quarter
    s, c = series(square, SIN) * quarter, series(square, COS)
    taps = []
    for r in range(8):
        x = (r - 3.0) - frac
        a = math.pi * (r - 3) / 4.0
        window = 0.5 + (0.5 * math.cos(a)) * c + (0.5 * math.sin(a)) * s
        tap = (scaled if r % 2 == 0 else -scaled) / x * window
        if r in (3, 4):
            tap = jnp.where(x == 0.0, weight, tap)
        taps.append(tap.astype(BF))
    return taps


def tile(mh, fc):
    return pl.ds(mh * 16, 16), pl.ds(fc * 128, 128)


def fill_taps(fw, taps):
    for mh in range(2):
        for fc in range(4):
            rows, cols = tile(mh, fc)
            for p, t in enumerate(eight_taps(fw[0, rows, cols], fw[1, rows, cols])):
                taps[p, rows, cols] = t


def coefficients(taps, delay):
    zero = jnp.zeros((16, 128), BF)
    columns = []
    for fc in range(4):
        parts = []
        for mh in range(2):
            rows, cols = tile(mh, fc)
            t = [taps[p, rows, cols] for p in range(8)]
            d = delay[rows, cols]
            at = [(d + I16(7 - q)) >> I16(3) for q in range(8)]
            for bit in (4, 2, 1):
                on = (d & I16(bit)) != I16(0)
                t = [jnp.where(on, t[(q - bit) % 8], t[q]) for q in range(8)]
            parts.append((t, at))
        columns.append(
            jnp.concatenate(
                [jnp.where(at[q] == I16(h), t[q], zero) for h in range(8) for q in range(8) for t, at in parts],
                axis=0,
            )
        )
    return jnp.concatenate(columns, axis=1)


def spread(sig, b, g, hh):
    s = sig[:, pl.ds(pl.multiple_of(b * SUB, 128), 384)].astype(F32)
    g[...] = jnp.concatenate([s] + [pltpu.roll(s, 384 - k, 1) for k in range(1, 4)], axis=0).T
    for k in range(4):
        hh[:, pl.ds(k * 128, 128)] = g[pl.ds(4 * k, 304), :].astype(BF)


def block_dot(hh, taps, delay):
    lhs = jnp.concatenate([hh[pl.ds(16 * k, SUB), :] for k in range(4)], axis=1)
    return jnp.dot(lhs, coefficients(taps, delay), preferred_element_type=F32)


def halves(wide, put):
    lane = lax.broadcasted_iota(jnp.int32, (MICS, 128), 1)
    for i in range(4):
        c0, c1 = wide(2 * i), wide(2 * i + 1)
        put(0, i, jnp.where(lane < 64, c0, pltpu.roll(c1, 64, 1)))
        put(1, i, jnp.where(lane < 64, pltpu.roll(c0, 64, 1), c1))


def kernel(signal, delay, fraction, weight, out,
           sig, psig, raw, dly, pdly, fwraw, fw, pfw, taps, ptaps, g, hh, own, part, sbuf, rbuf,
           lsem, xs, xr, ds_, dr, gs, gr, hs, hr, ss, rs):
    mic, tm = lax.axis_index("mic"), lax.axis_index("tm")
    z, h = mic // 2, lax.rem(mic, 2)
    other = z * 2 + 1 - h
    right = lax.rem(z + 1, RING) * 2 + h
    left = lax.rem(z + RING - 1, RING) * 2 + h
    ntm = lax.axis_size("tm")

    bar = pltpu.get_barrier_semaphore()
    for peer in (other, right, left):
        pl.semaphore_signal(bar, inc=1, device_id={"mic": peer, "tm": tm}, device_id_type=MESH)

    @pl.when(tm < ntm - 1)
    def _():
        for peer in (mic, other):
            pl.semaphore_signal(bar, inc=1, device_id={"mic": peer, "tm": tm + 1}, device_id_type=MESH)

    loads = [
        pltpu.make_async_copy(fraction, fwraw.at[0], lsem.at[0]),
        pltpu.make_async_copy(weight, fwraw.at[1], lsem.at[1]),
        pltpu.make_async_copy(delay.at[0], raw.at[0], lsem.at[2]),
        pltpu.make_async_copy(signal, sig.at[:, pl.ds(0, TIME)], lsem.at[3]),
        pltpu.make_async_copy(delay.at[pl.ds(1, NB - 1)], raw.at[pl.ds(1, NB - 1)], lsem.at[4]),
    ]
    for c in loads:
        c.start()

    @pl.when(tm == ntm - 1)
    def _():
        sig[:, pl.ds(TIME, 128)] = jnp.zeros((MICS, 128), BF)
        psig[:, pl.ds(TIME, 128)] = jnp.zeros((MICS, 128), BF)

    def remote(src, dst, send, recv, **to):
        return pltpu.make_async_remote_copy(src, dst, send, recv, device_id={"mic": mic, "tm": tm, **to}, device_id_type=MESH)

    def send_fw():
        return remote(fw.at[1 - h], pfw, gs, gr, mic=other)

    def send_delay(b):
        return remote(dly.at[1 - h, b], pdly.at[b], ds_.at[b], dr.at[b], mic=other)

    def send_piece(c):
        cols = pl.ds(pl.multiple_of(c * SUB, 128), SUB)
        return remote(sig.at[:, cols], psig.at[:, cols], xs.at[c], xr.at[c], mic=other)

    def send_halo(k):
        dst = (sig, psig)[k]
        peer = (mic, other)[k]
        return remote(sig.at[:, pl.ds(0, 128)], dst.at[:, pl.ds(TIME, 128)], hs.at[k], hr.at[k], mic=peer, tm=tm - 1)

    def wait_halo(k):
        dst = (sig, psig)[k]
        remote(sig.at[:, pl.ds(0, 128)], dst.at[:, pl.ds(TIME, 128)], hs.at[k], hr.at[k]).wait_recv()

    loads[0].wait()
    loads[1].wait()
    for k in range(2):
        def put(half, i, v, k=k):
            fw[half, k, :, pl.ds(i * 128, 128)] = v
        halves(lambda i, k=k: fwraw[k, :, pl.ds(i * 128, 128)], put)

    def compact(b):
        def put(half, i, v):
            dly[half, b, :, pl.ds(i * 128, 128)] = v.astype(I16)
        halves(lambda i: raw[b, :, pl.ds(i * 128, 128)], put)

    loads[2].wait()
    compact(0)
    loads[3].wait()

    @pl.when(tm > 0)
    def _():
        pl.semaphore_wait(bar, 5)

    @pl.when(tm == 0)
    def _():
        pl.semaphore_wait(bar, 3)

    send_fw().start()
    send_delay(0).start()
    send_piece(0).start()
    send_piece(1).start()

    @pl.when(tm > 0)
    def _():
        send_halo(0).start()
        send_halo(1).start()

    loads[4].wait()

    @pl.loop(1, NB)
    def _(b):
        compact(b)
        send_delay(b).start()

        @pl.when(b < NB - 1)
        def _():
            send_piece(b + 1).start()

    fill_taps(fw.at[h], taps)

    @pl.loop(0, NB)
    def _(b):
        @pl.when((b == NB - 1) & (tm < ntm - 1))
        def _():
            wait_halo(0)

        spread(sig, b, g, hh)
        own[b] = block_dot(hh, taps, dly.at[h, b])

    send_fw().wait_recv()
    fill_taps(pfw, ptaps)
    send_piece(0).wait_recv()

    lane = lax.broadcasted_iota(jnp.int32, (128, 128), 1)

    def message(b, way, hop):
        peer = (right, left)[way]
        return remote(sbuf.at[way, b, hop], rbuf.at[way, b, hop], ss.at[way, b, hop], rs.at[way, b, hop], mic=peer)

    def length(odd, way):
        return 4 if odd == way else 3

    def hop(pair, k):
        for odd in range(2):
            for way in range(2):
                steps = length(odd, way)
                if k >= steps:
                    continue
                b = 2 * pair + odd
                ahead = steps - k
                dest = lax.rem(z + (ahead if way == 0 else RING - ahead), RING)
                total = part[b, dest]
                if k > 0:
                    message(b, way, k - 1).wait_recv()
                    total = total + rbuf[way, b, k - 1].astype(F32)
                sbuf[way, b, k] = total.astype(BF)
                message(b, way, k).start()

    def finish(pair):
        for odd in range(2):
            b = 2 * pair + odd
            total = part[b, z]
            for way in range(2):
                last = length(odd, way) - 1
                message(b, way, last).wait_recv()
                total = total + rbuf[way, b, last].astype(F32)
            flat = total.T
            start = pl.multiple_of(b * SUB, 128)
            out[:, pl.ds(start, 128)] = flat[0:64, :]
            out[:, pl.ds(pl.multiple_of(start + 128, 128), 128)] = flat[64:128, :]

    def form(b):
        spread(psig, b, g, hh)
        r = own[b] + block_dot(hh, ptaps, pdly.at[b])
        for i in range(4):
            top, bottom = r[0:128, i * 128 : i * 128 + 128], r[128:256, i * 128 : i * 128 + 128]
            part[b, 2 * i] = jnp.where(lane < 64, top, pltpu.roll(bottom, 64, 1))
            part[b, 2 * i + 1] = jnp.where(lane < 64, pltpu.roll(top, 64, 1), bottom)

    @pl.loop(0, 8)
    def _(i):
        @pl.when(i < 4)
        def _():
            send_delay(2 * i).wait_recv()
            send_piece(2 * i + 1).wait_recv()
            form(2 * i)
            send_delay(2 * i + 1).wait_recv()

            @pl.when(i < 3)
            def _():
                send_piece(2 * i + 2).wait_recv()

            @pl.when((i == 3) & (tm < ntm - 1))
            def _():
                wait_halo(1)

            form(2 * i + 1)
            hop(i, 0)

        for k in (3, 2, 1):
            @pl.when((i >= k) & (i < 4 + k))
            def _(k=k):
                hop(i - k, k)

        @pl.when(i >= 4)
        def _():
            finish(i - 4)

    send_fw().wait_send()

    @pl.loop(0, NB)
    def _(b):
        send_delay(b).wait_send()
        send_piece(b).wait_send()

    @pl.when(tm > 0)
    def _():
        send_halo(0).wait_send()
        send_halo(1).wait_send()

    @pl.loop(0, NB // 2)
    def _(i):
        for odd in range(2):
            for way in range(2):
                for k in range(length(odd, way)):
                    message(2 * i + odd, way, k).wait_send()


def shards(signal, delay, fraction, weight):
    dma = pltpu.SemaphoreType.DMA
    return pl.pallas_call(
        kernel,
        out_shape=jax.ShapeDtypeStruct((FOCUS // 16, TIME), F32),
        in_specs=[pl.BlockSpec(memory_space=pl.ANY)] * 4,
        out_specs=pl.BlockSpec(memory_space=pltpu.VMEM),
        scratch_shapes=[
            pltpu.VMEM((MICS, WIDE), BF),
            pltpu.VMEM((MICS, WIDE), BF),
            pltpu.VMEM((NB, MICS, FOCUS), jnp.int32),
            pltpu.VMEM((2, NB, MICS, HALF), I16),
            pltpu.VMEM((NB, MICS, HALF), I16),
            pltpu.VMEM((2, MICS, FOCUS), F32),
            pltpu.VMEM((2, 2, MICS, HALF), F32),
            pltpu.VMEM((2, MICS, HALF), F32),
            pltpu.VMEM((8, MICS, HALF), BF),
            pltpu.VMEM((8, MICS, HALF), BF),
            pltpu.VMEM((384, 128), F32),
            pltpu.VMEM((304, 512), BF),
            pltpu.VMEM((NB, SUB, HALF), F32),
            pltpu.VMEM((NB, RING, 128, 128), F32),
            pltpu.VMEM((2, NB, 4, 128, 128), BF),
            pltpu.VMEM((2, NB, 4, 128, 128), BF),
            dma((5,)),
            dma((NB,)), dma((NB,)),
            dma((NB,)), dma((NB,)),
            dma, dma,
            dma((2,)), dma((2,)),
            dma((2, NB, 4)), dma((2, NB, 4)),
        ],
        compiler_params=pltpu.CompilerParams(
            collective_id=0, has_side_effects=True, vmem_limit_bytes=48 * 1024 * 1024
        ),
    )(signal, delay, fraction, weight)


def solution(mesh):
    return jax.shard_map(
        shards,
        mesh=mesh,
        in_specs=(P("mic", "tm"), P("tm", "mic", None), P("mic", None), P("mic", None)),
        out_specs=P("mic", "tm"),
        check_vma=False,
    )
```

```python
import math

import jax
import jax.numpy as jnp
from jax import lax
from jax.experimental import pallas as pl
from jax.experimental.pallas import tpu as pltpu
from jax.sharding import PartitionSpec as P

MESH = pl.DeviceIdType.MESH
BF, F32, I16 = jnp.bfloat16, jnp.float32, jnp.int16
MICS, FOCUS, HALF, NB, SUB, TIME = 32, 1024, 512, 8, 256, 2048
RING = 8
WIDE = TIME + 128


def series(y, terms):
    r = jnp.full_like(y, terms[-1])
    for c in terms[-2::-1]:
        r = r * y + c
    return r


SIN = [(-1) ** k * math.pi ** (2 * k + 1) / math.factorial(2 * k + 1) for k in range(7)]
COS = [(-1) ** k * math.pi ** (2 * k) / math.factorial(2 * k) for k in range(6)]


def eight_taps(frac, weight):
    low = jnp.minimum(frac, 1.0 - frac)
    scaled = series(low * low, SIN) * low * weight * (1.0 / math.pi)
    quarter = frac * 0.25
    square = quarter * quarter
    s, c = series(square, SIN) * quarter, series(square, COS)
    taps = []
    for r in range(8):
        x = (r - 3.0) - frac
        a = math.pi * (r - 3) / 4.0
        window = 0.5 + (0.5 * math.cos(a)) * c + (0.5 * math.sin(a)) * s
        tap = (scaled if r % 2 == 0 else -scaled) / x * window
        if r in (3, 4):
            tap = jnp.where(x == 0.0, weight, tap)
        taps.append(tap.astype(BF))
    return taps


def tile(mh, fc):
    return pl.ds(mh * 16, 16), pl.ds(fc * 128, 128)


def fill_taps(fw, taps):
    for mh in range(2):
        for fc in range(4):
            rows, cols = tile(mh, fc)
            for p, t in enumerate(eight_taps(fw[0, rows, cols], fw[1, rows, cols])):
                taps[p, rows, cols] = t


def coefficients(taps, delay):
    zero = jnp.zeros((16, 128), BF)
    columns = []
    for fc in range(4):
        parts = []
        for mh in range(2):
            rows, cols = tile(mh, fc)
            t = [taps[p, rows, cols] for p in range(8)]
            d = delay[rows, cols]
            row, column = (d >> I16(3)).astype(BF), (d & I16(7)).astype(BF)
            after = row + BF(1)
            at = [jnp.where(column > BF(q), after, row) for q in range(8)]
            for bit in (4, 2, 1):
                on = (d & I16(bit)).astype(BF) != BF(0)
                t = [jnp.where(on, t[(q - bit) % 8], t[q]) for q in range(8)]
            parts.append((t, at))
        columns.append(
            jnp.concatenate(
                [jnp.where(at[q] == BF(h), t[q], zero) for h in range(8) for q in range(8) for t, at in parts],
                axis=0,
            )
        )
    return jnp.concatenate(columns, axis=1)


def spread(sig, pair, g, hh):
    s = sig[:, pl.ds(pl.multiple_of(pair * 2 * SUB, 128), 640)].astype(F32)
    g[...] = jnp.concatenate([s] + [pltpu.roll(s, 640 - k, 1) for k in range(1, 4)], axis=0).T
    for k in range(4):
        hh[:, pl.ds(k * 128, 128)] = g[pl.ds(4 * k, 2 * SUB + 48), :].astype(BF)


def block_dot(hh, odd, taps, delay):
    lhs = jnp.concatenate([hh[pl.ds(SUB * odd + 16 * k, SUB), :] for k in range(4)], axis=1)
    return jnp.dot(lhs, coefficients(taps, delay), preferred_element_type=F32)


def halves(wide, put):
    lane = lax.broadcasted_iota(jnp.int32, (MICS, 128), 1)
    for i in range(4):
        c0, c1 = wide(2 * i), wide(2 * i + 1)
        put(0, i, jnp.where(lane < 64, c0, pltpu.roll(c1, 64, 1)))
        put(1, i, jnp.where(lane < 64, pltpu.roll(c0, 64, 1), c1))


def kernel(signal, delay, fraction, weight, out,
           sig, psig, raw, dly, pdly, fwraw, fw, pfw, taps, ptaps, g, hh, own, part, sbuf, rbuf,
           lsem, xs, xr, ds_, dr, gs, gr, hs, hr, ss, rs):
    mic, tm = lax.axis_index("mic"), lax.axis_index("tm")
    z, h = mic // 2, lax.rem(mic, 2)
    other = z * 2 + 1 - h
    right = lax.rem(z + 1, RING) * 2 + h
    left = lax.rem(z + RING - 1, RING) * 2 + h
    ntm = lax.axis_size("tm")

    bar = pltpu.get_barrier_semaphore()
    core = lax.rem(tm, 2)
    sibling = tm + 1 - 2 * core
    for peer, at in ((other, tm), (right, tm), (left, tm), (mic, sibling)):
        pl.semaphore_signal(bar, inc=1, device_id={"mic": peer, "tm": at}, device_id_type=MESH)

    @pl.when(tm < ntm - 1)
    def _():
        for peer in (mic, other):
            pl.semaphore_signal(bar, inc=1, device_id={"mic": peer, "tm": tm + 1}, device_id_type=MESH)

    loads = [
        pltpu.make_async_copy(fraction, fwraw.at[0], lsem.at[0]),
        pltpu.make_async_copy(weight, fwraw.at[1], lsem.at[1]),
        pltpu.make_async_copy(delay.at[0], raw.at[0], lsem.at[2]),
        pltpu.make_async_copy(signal, sig.at[:, pl.ds(0, TIME)], lsem.at[3]),
        pltpu.make_async_copy(delay.at[pl.ds(1, NB - 1)], raw.at[pl.ds(1, NB - 1)], lsem.at[4]),
    ]
    for c in loads:
        c.start()

    @pl.when(tm == ntm - 1)
    def _():
        sig[:, pl.ds(TIME, 128)] = jnp.zeros((MICS, 128), BF)
        psig[:, pl.ds(TIME, 128)] = jnp.zeros((MICS, 128), BF)

    def remote(src, dst, send, recv, **to):
        return pltpu.make_async_remote_copy(src, dst, send, recv, device_id={"mic": mic, "tm": tm, **to}, device_id_type=MESH)

    def send_fw():
        return remote(fw.at[1 - h, core], pfw.at[core], gs.at[0], gr.at[0], mic=other)

    def share_fw():
        return remote(pfw.at[core], pfw.at[core], gs.at[1], gr.at[1], tm=sibling)

    def send_delay(b):
        return remote(dly.at[1 - h, b], pdly.at[b], ds_.at[b], dr.at[b], mic=other)

    def send_piece(c):
        cols = pl.ds(pl.multiple_of(c * SUB, 128), SUB)
        return remote(sig.at[:, cols], psig.at[:, cols], xs.at[c], xr.at[c], mic=other)

    def send_halo(k):
        dst = (sig, psig)[k]
        peer = (mic, other)[k]
        return remote(sig.at[:, pl.ds(0, 128)], dst.at[:, pl.ds(TIME, 128)], hs.at[k], hr.at[k], mic=peer, tm=tm - 1)

    def wait_halo(k):
        dst = (sig, psig)[k]
        remote(sig.at[:, pl.ds(0, 128)], dst.at[:, pl.ds(TIME, 128)], hs.at[k], hr.at[k]).wait_recv()

    loads[0].wait()
    loads[1].wait()
    for k in range(2):
        def put(half, i, v, k=k):
            fw[half, k, :, pl.ds(i * 128, 128)] = v
        halves(lambda i, k=k: fwraw[k, :, pl.ds(i * 128, 128)], put)

    def compact(b):
        def put(half, i, v):
            dly[half, b, :, pl.ds(i * 128, 128)] = v.astype(I16)
        halves(lambda i: raw[b, :, pl.ds(i * 128, 128)], put)

    loads[2].wait()
    compact(0)
    loads[3].wait()

    @pl.when(tm > 0)
    def _():
        pl.semaphore_wait(bar, 6)

    @pl.when(tm == 0)
    def _():
        pl.semaphore_wait(bar, 4)

    send_fw().start()
    send_delay(0).start()
    send_piece(0).start()
    send_piece(1).start()
    loads[4].wait()

    @pl.loop(1, NB)
    def _(b):
        compact(b)
        send_delay(b).start()

        @pl.when(b < NB - 1)
        def _():
            send_piece(b + 1).start()

        @pl.when((b == 2) & (tm > 0))
        def _():
            send_halo(0).start()
            send_halo(1).start()

    fill_taps(fw.at[h], taps)

    @pl.loop(0, NB // 2)
    def _(i):
        @pl.when((i == NB // 2 - 1) & (tm < ntm - 1))
        def _():
            wait_halo(0)

        @pl.when(i == 2)
        def _():
            send_fw().wait_recv()
            share_fw().start()

        spread(sig, i, g, hh)
        for odd in range(2):
            own[2 * i + odd] = block_dot(hh, odd, taps, dly.at[h, 2 * i + odd])

    share_fw().wait_recv()
    fill_taps(pfw, ptaps)
    send_piece(0).wait_recv()

    lane = lax.broadcasted_iota(jnp.int32, (128, 128), 1)

    def message(b, way, hop):
        peer = (right, left)[way]
        return remote(sbuf.at[way, b, hop], rbuf.at[way, b, hop], ss.at[way, b, hop], rs.at[way, b, hop], mic=peer)

    def length(odd, way):
        return 4 if odd == way else 3

    def hop(pair, k):
        for odd in range(2):
            for way in range(2):
                steps = length(odd, way)
                if k >= steps:
                    continue
                b = 2 * pair + odd
                ahead = steps - k
                dest = lax.rem(z + (ahead if way == 0 else RING - ahead), RING)
                total = part[b, dest]
                if k > 0:
                    message(b, way, k - 1).wait_recv()
                    total = total + rbuf[way, b, k - 1].astype(F32)
                sbuf[way, b, k] = total.astype(BF)
                message(b, way, k).start()

    def finish(pair):
        for odd in range(2):
            b = 2 * pair + odd
            total = part[b, z]
            for way in range(2):
                last = length(odd, way) - 1
                message(b, way, last).wait_recv()
                total = total + rbuf[way, b, last].astype(F32)
            flat = total.T
            start = pl.multiple_of(b * SUB, 128)
            out[:, pl.ds(start, 128)] = flat[0:64, :]
            out[:, pl.ds(pl.multiple_of(start + 128, 128), 128)] = flat[64:128, :]

    def form(pair):
        spread(psig, pair, g, hh)
        for odd in range(2):
            b = 2 * pair + odd
            r = own[b] + block_dot(hh, odd, ptaps, pdly.at[b])
            for i in range(4):
                top, bottom = r[0:128, i * 128 : i * 128 + 128], r[128:256, i * 128 : i * 128 + 128]
                part[b, 2 * i] = jnp.where(lane < 64, top, pltpu.roll(bottom, 64, 1))
                part[b, 2 * i + 1] = jnp.where(lane < 64, pltpu.roll(top, 64, 1), bottom)

    @pl.loop(0, NB // 2)
    def _(i):
        send_delay(2 * i).wait_recv()
        send_piece(2 * i + 1).wait_recv()
        send_delay(2 * i + 1).wait_recv()

        @pl.when(i < NB // 2 - 1)
        def _():
            send_piece(2 * i + 2).wait_recv()

        @pl.when((i == NB // 2 - 1) & (tm < ntm - 1))
        def _():
            wait_halo(1)

        form(i)
        hop(i, 0)

        @pl.when(i > 0)
        def _():
            hop(i - 1, 1)

    hop(0, 2)
    hop(3, 1)

    @pl.loop(1, NB // 2)
    def _(i):
        hop(i, 2)

    @pl.loop(0, NB // 2)
    def _(i):
        hop(i, 3)

    @pl.loop(0, NB // 2)
    def _(i):
        finish(i)

    send_fw().wait_send()
    share_fw().wait_send()

    @pl.loop(0, NB)
    def _(b):
        send_delay(b).wait_send()
        send_piece(b).wait_send()

    @pl.when(tm > 0)
    def _():
        send_halo(0).wait_send()
        send_halo(1).wait_send()

    @pl.loop(0, NB // 2)
    def _(i):
        for odd in range(2):
            for way in range(2):
                for k in range(length(odd, way)):
                    message(2 * i + odd, way, k).wait_send()


def shards(signal, delay, fraction, weight):
    dma = pltpu.SemaphoreType.DMA
    return pl.pallas_call(
        kernel,
        out_shape=jax.ShapeDtypeStruct((FOCUS // 16, TIME), F32),
        in_specs=[pl.BlockSpec(memory_space=pltpu.HBM)] * 4,
        out_specs=pl.BlockSpec(memory_space=pltpu.VMEM),
        scratch_shapes=[
            pltpu.VMEM((MICS, WIDE), BF),
            pltpu.VMEM((MICS, WIDE), BF),
            pltpu.VMEM((NB, MICS, FOCUS), jnp.int32),
            pltpu.VMEM((2, NB, MICS, HALF), I16),
            pltpu.VMEM((NB, MICS, HALF), I16),
            pltpu.VMEM((2, MICS, FOCUS), F32),
            pltpu.VMEM((2, 2, MICS, HALF), F32),
            pltpu.VMEM((2, MICS, HALF), F32),
            pltpu.VMEM((8, MICS, HALF), BF),
            pltpu.VMEM((8, MICS, HALF), BF),
            pltpu.VMEM((640, 128), F32),
            pltpu.VMEM((2 * SUB + 48, 512), BF),
            pltpu.VMEM((NB, SUB, HALF), F32),
            pltpu.VMEM((NB, RING, 128, 128), F32),
            pltpu.VMEM((2, NB, 4, 128, 128), BF),
            pltpu.VMEM((2, NB, 4, 128, 128), BF),
            dma((5,)),
            dma((NB,)), dma((NB,)),
            dma((NB,)), dma((NB,)),
            dma((2,)), dma((2,)),
            dma((2,)), dma((2,)),
            dma((2, NB, 4)), dma((2, NB, 4)),
        ],
        compiler_params=pltpu.CompilerParams(
            collective_id=0, has_side_effects=True, vmem_limit_bytes=60 * 1024 * 1024
        ),
    )(signal, delay, fraction, weight)


def solution(mesh):
    return jax.shard_map(
        shards,
        mesh=mesh,
        in_specs=(P("mic", "tm"), P("tm", "mic", None), P("mic", None), P("mic", None)),
        out_specs=P("mic", "tm"),
        check_vma=False,
    )
```

```python
import math

import jax
import jax.numpy as jnp
from jax import lax
from jax.experimental import pallas as pl
from jax.experimental.pallas import tpu as pltpu
from jax.sharding import PartitionSpec as P

MESH = pl.DeviceIdType.MESH
BF, F32, I16 = jnp.bfloat16, jnp.float32, jnp.int16
MICS, FOCUS, HALF, NB, SUB, TIME = 32, 1024, 512, 8, 256, 2048
RING = 8
WIDE = TIME + 128


def series(y, terms):
    r = jnp.full_like(y, terms[-1])
    for c in terms[-2::-1]:
        r = r * y + c
    return r


SIN = [(-1) ** k * math.pi ** (2 * k + 1) / math.factorial(2 * k + 1) for k in range(7)]
COS = [(-1) ** k * math.pi ** (2 * k) / math.factorial(2 * k) for k in range(6)]


def eight_taps(frac, weight):
    low = jnp.minimum(frac, 1.0 - frac)
    scaled = series(low * low, SIN) * low * weight * (1.0 / math.pi)
    quarter = frac * 0.25
    square = quarter * quarter
    s, c = series(square, SIN) * quarter, series(square, COS)
    taps = []
    for r in range(8):
        x = (r - 3.0) - frac
        a = math.pi * (r - 3) / 4.0
        window = 0.5 + (0.5 * math.cos(a)) * c + (0.5 * math.sin(a)) * s
        tap = (scaled if r % 2 == 0 else -scaled) / x * window
        if r in (3, 4):
            tap = jnp.where(x == 0.0, weight, tap)
        taps.append(tap.astype(BF))
    return taps


def tile(mh, fc):
    return pl.ds(mh * 16, 16), pl.ds(fc * 128, 128)


def fill_taps(fw, taps):
    for mh in range(2):
        for fc in range(4):
            rows, cols = tile(mh, fc)
            for p, t in enumerate(eight_taps(fw[0, rows, cols], fw[1, rows, cols])):
                taps[p, rows, cols] = t


def coefficients(taps, delay):
    zero = jnp.zeros((16, 128), BF)
    columns = []
    for fc in range(4):
        parts = []
        for mh in range(2):
            rows, cols = tile(mh, fc)
            t = [taps[p, rows, cols] for p in range(8)]
            d = delay[rows, cols]
            row, column = (d >> I16(3)).astype(BF), (d & I16(7)).astype(BF)
            after = row + BF(1)
            at = [jnp.where(column > BF(q), after, row) for q in range(8)]
            for bit in (4, 2, 1):
                on = (d & I16(bit)).astype(BF) != BF(0)
                t = [jnp.where(on, t[(q - bit) % 8], t[q]) for q in range(8)]
            parts.append((t, at))
        columns.append(
            jnp.concatenate(
                [jnp.where(at[q] == BF(h), t[q], zero) for h in range(8) for q in range(8) for t, at in parts],
                axis=0,
            )
        )
    return jnp.concatenate(columns, axis=1)


def spread(sig, first, blocks, g, hh):
    wide = SUB * blocks + 128
    s = sig[:, pl.ds(pl.multiple_of(first * SUB, 128), wide)].astype(F32)
    g[pl.ds(0, wide), :] = jnp.concatenate([s] + [pltpu.roll(s, wide - k, 1) for k in range(1, 4)], axis=0).T
    rows = SUB * blocks + 48
    for k in range(4):
        hh[pl.ds(0, rows), pl.ds(k * 128, 128)] = g[pl.ds(4 * k, rows), :].astype(BF)


def block_dot(hh, odd, taps, delay):
    lhs = jnp.concatenate([hh[pl.ds(SUB * odd + 16 * k, SUB), :] for k in range(4)], axis=1)
    return jnp.dot(lhs, coefficients(taps, delay), preferred_element_type=F32)


def halves(wide, put):
    lane = lax.broadcasted_iota(jnp.int32, (MICS, 128), 1)
    for i in range(4):
        c0, c1 = wide(2 * i), wide(2 * i + 1)
        put(0, i, jnp.where(lane < 64, c0, pltpu.roll(c1, 64, 1)))
        put(1, i, jnp.where(lane < 64, pltpu.roll(c0, 64, 1), c1))


def kernel(signal, delay, fraction, weight, out,
           sig, psig, raw, dly, pdly, fwraw, fw, pfw, taps, ptaps, g, hh, own, part, sbuf, rbuf, outv,
           lsem, xs, xr, ds_, dr, gs, gr, hs, hr, ss, rs):
    mic, tm = lax.axis_index("mic"), lax.axis_index("tm")
    z, h = mic // 2, lax.rem(mic, 2)
    other = z * 2 + 1 - h
    right = lax.rem(z + 1, RING) * 2 + h
    left = lax.rem(z + RING - 1, RING) * 2 + h
    ntm = lax.axis_size("tm")

    bar = pltpu.get_barrier_semaphore()
    core = lax.rem(tm, 2)
    sibling = tm + 1 - 2 * core
    for peer, at in ((other, tm), (right, tm), (left, tm), (mic, sibling)):
        pl.semaphore_signal(bar, inc=1, device_id={"mic": peer, "tm": at}, device_id_type=MESH)

    @pl.when(tm < ntm - 1)
    def _():
        for peer in (mic, other):
            pl.semaphore_signal(bar, inc=1, device_id={"mic": peer, "tm": tm + 1}, device_id_type=MESH)

    loads = [
        pltpu.make_async_copy(fraction, fwraw.at[0], lsem.at[0]),
        pltpu.make_async_copy(weight, fwraw.at[1], lsem.at[1]),
        pltpu.make_async_copy(delay.at[0], raw.at[0], lsem.at[2]),
        pltpu.make_async_copy(signal, sig.at[:, pl.ds(0, TIME)], lsem.at[3]),
        pltpu.make_async_copy(delay.at[pl.ds(1, NB - 1)], raw.at[pl.ds(1, NB - 1)], lsem.at[4]),
    ]
    for c in loads:
        c.start()

    @pl.when(tm == ntm - 1)
    def _():
        sig[:, pl.ds(TIME, 128)] = jnp.zeros((MICS, 128), BF)
        psig[:, pl.ds(TIME, 128)] = jnp.zeros((MICS, 128), BF)

    def remote(src, dst, send, recv, **to):
        return pltpu.make_async_remote_copy(src, dst, send, recv, device_id={"mic": mic, "tm": tm, **to}, device_id_type=MESH)

    def send_fw():
        return remote(fw.at[1 - h, core], pfw.at[core], gs.at[0], gr.at[0], mic=other)

    def share_fw():
        return remote(pfw.at[core], pfw.at[core], gs.at[1], gr.at[1], tm=sibling)

    def send_delay(b):
        return remote(dly.at[1 - h, b], pdly.at[b], ds_.at[b], dr.at[b], mic=other)

    def send_piece(c):
        cols = pl.ds(pl.multiple_of(c * SUB, 128), SUB)
        return remote(sig.at[:, cols], psig.at[:, cols], xs.at[c], xr.at[c], mic=other)

    def send_halo(k):
        dst = (sig, psig)[k]
        peer = (mic, other)[k]
        return remote(sig.at[:, pl.ds(0, 128)], dst.at[:, pl.ds(TIME, 128)], hs.at[k], hr.at[k], mic=peer, tm=tm - 1)

    def wait_halo(k):
        dst = (sig, psig)[k]
        remote(sig.at[:, pl.ds(0, 128)], dst.at[:, pl.ds(TIME, 128)], hs.at[k], hr.at[k]).wait_recv()

    loads[0].wait()
    loads[1].wait()
    for k in range(2):
        def put(half, i, v, k=k):
            fw[half, k, :, pl.ds(i * 128, 128)] = v
        halves(lambda i, k=k: fwraw[k, :, pl.ds(i * 128, 128)], put)

    def compact(b):
        def put(half, i, v):
            dly[half, b, :, pl.ds(i * 128, 128)] = v.astype(I16)
        halves(lambda i: raw[b, :, pl.ds(i * 128, 128)], put)

    loads[2].wait()
    compact(0)
    loads[3].wait()

    @pl.when(tm > 0)
    def _():
        pl.semaphore_wait(bar, 6)

    @pl.when(tm == 0)
    def _():
        pl.semaphore_wait(bar, 4)

    send_fw().start()
    send_delay(0).start()
    send_piece(0).start()
    send_piece(1).start()
    loads[4].wait()

    def pass_on(b):
        compact(b)
        send_delay(b).start()

        @pl.when(b < NB - 1)
        def _():
            send_piece(b + 1).start()

    pass_on(1)
    pass_on(2)

    @pl.when(tm > 0)
    def _():
        send_halo(0).start()
        send_halo(1).start()

    fill_taps(fw.at[h], taps)

    def half(pair):
        spread(sig, 2 * pair, 2, g, hh)
        for odd in range(2):
            own[2 * pair + odd] = block_dot(hh, odd, taps, dly.at[h, 2 * pair + odd])

    @pl.loop(0, 2)
    def _(i):
        half(i)
        pass_on(2 * i + 3)
        pass_on(2 * i + 4)

    send_fw().wait_recv()
    share_fw().start()
    pass_on(NB - 1)
    share_fw().wait_recv()
    fill_taps(pfw, ptaps)
    send_piece(0).wait_recv()

    lane = lax.broadcasted_iota(jnp.int32, (128, 128), 1)

    def message(b, way, hop):
        peer = (right, left)[way]
        return remote(sbuf.at[way, b, hop], rbuf.at[way, b, hop], ss.at[way, b, hop], rs.at[way, b, hop], mic=peer)

    def length(odd, way):
        return 4 if odd == way else 3

    def hop(pair, odd, k):
        for way in range(2):
            steps = length(odd, way)
            if k >= steps:
                continue
            b = 2 * pair + odd
            ahead = steps - k
            dest = lax.rem(z + (ahead if way == 0 else RING - ahead), RING)
            total = part[b, dest]
            if k > 0:
                message(b, way, k - 1).wait_recv()
                total = total + rbuf[way, b, k - 1].astype(F32)
            sbuf[way, b, k] = total.astype(BF)
            message(b, way, k).start()

    def deliver(b):
        cols = pl.ds(pl.multiple_of(b * SUB, 128), SUB)
        return pltpu.make_async_copy(outv.at[:, cols], out.at[:, cols], lsem.at[5 + b])

    def finish(pair):
        for odd in range(2):
            b = 2 * pair + odd
            total = part[b, z]
            for way in range(2):
                last = length(odd, way) - 1
                message(b, way, last).wait_recv()
                total = total + rbuf[way, b, last].astype(F32)
            flat = total.T
            start = pl.multiple_of(b * SUB, 128)
            outv[:, pl.ds(start, 128)] = flat[0:64, :]
            outv[:, pl.ds(pl.multiple_of(start + 128, 128), 128)] = flat[64:128, :]
            deliver(b).start()

    def form(first, blocks):
        spread(psig, first, blocks, g, hh)
        for odd in range(blocks):
            b = first + odd
            r = own[b] + block_dot(hh, odd, ptaps, pdly.at[b])
            for i in range(4):
                top, bottom = r[0:128, i * 128 : i * 128 + 128], r[128:256, i * 128 : i * 128 + 128]
                part[b, 2 * i] = jnp.where(lane < 64, top, pltpu.roll(bottom, 64, 1))
                part[b, 2 * i + 1] = jnp.where(lane < 64, pltpu.roll(top, 64, 1), bottom)

    last = NB // 2 - 1

    @pl.loop(0, 2)
    def _(b):
        send_delay(b).wait_recv()
        send_piece(b + 1).wait_recv()
        form(b, 1)

        for odd in range(2):
            @pl.when(b == odd)
            def _(odd=odd):
                hop(0, odd, 0)

    @pl.loop(1, NB // 2)
    def _(i):
        @pl.when((i == last) & (tm < ntm - 1))
        def _():
            wait_halo(0)

        @pl.when(i >= 2)
        def _():
            half(i)
            for odd in range(2):
                hop(i - 2, odd, 1)

        send_delay(2 * i).wait_recv()
        send_piece(2 * i + 1).wait_recv()
        send_delay(2 * i + 1).wait_recv()

        @pl.when(i < last)
        def _():
            send_piece(2 * i + 2).wait_recv()

        @pl.when((i == last) & (tm < ntm - 1))
        def _():
            wait_halo(1)

        form(2 * i, 2)
        for odd in range(2):
            hop(i, odd, 0)
    for odd in range(2):
        hop(last - 1, odd, 1)
    for odd in range(2):
        hop(0, odd, 2)
    for odd in range(2):
        hop(last, odd, 1)

    @pl.loop(1, NB // 2)
    def _(i):
        for odd in range(2):
            hop(i, odd, 2)

    @pl.loop(0, NB // 2)
    def _(i):
        for odd in range(2):
            hop(i, odd, 3)

    @pl.loop(0, NB // 2)
    def _(i):
        finish(i)

    send_fw().wait_send()
    share_fw().wait_send()

    @pl.loop(0, NB)
    def _(b):
        send_delay(b).wait_send()
        send_piece(b).wait_send()

    @pl.when(tm > 0)
    def _():
        send_halo(0).wait_send()
        send_halo(1).wait_send()

    @pl.loop(0, NB // 2)
    def _(i):
        for odd in range(2):
            for way in range(2):
                for k in range(length(odd, way)):
                    message(2 * i + odd, way, k).wait_send()
            deliver(2 * i + odd).wait()


def shards(signal, delay, fraction, weight):
    dma = pltpu.SemaphoreType.DMA
    return pl.pallas_call(
        kernel,
        out_shape=jax.ShapeDtypeStruct((FOCUS // 16, TIME), F32),
        in_specs=[pl.BlockSpec(memory_space=pltpu.HBM)] * 4,
        out_specs=pl.BlockSpec(memory_space=pltpu.HBM),
        scratch_shapes=[
            pltpu.VMEM((MICS, WIDE), BF),
            pltpu.VMEM((MICS, WIDE), BF),
            pltpu.VMEM((NB, MICS, FOCUS), jnp.int32),
            pltpu.VMEM((2, NB, MICS, HALF), I16),
            pltpu.VMEM((NB, MICS, HALF), I16),
            pltpu.VMEM((2, MICS, FOCUS), F32),
            pltpu.VMEM((2, 2, MICS, HALF), F32),
            pltpu.VMEM((2, MICS, HALF), F32),
            pltpu.VMEM((8, MICS, HALF), BF),
            pltpu.VMEM((8, MICS, HALF), BF),
            pltpu.VMEM((640, 128), F32),
            pltpu.VMEM((2 * SUB + 48, 512), BF),
            pltpu.VMEM((NB, SUB, HALF), F32),
            pltpu.VMEM((NB, RING, 128, 128), F32),
            pltpu.VMEM((2, NB, 4, 128, 128), BF),
            pltpu.VMEM((2, NB, 4, 128, 128), BF),
            pltpu.VMEM((FOCUS // 16, TIME), F32),
            dma((5 + NB,)),
            dma((NB,)), dma((NB,)),
            dma((NB,)), dma((NB,)),
            dma((2,)), dma((2,)),
            dma((2,)), dma((2,)),
            dma((2, NB, 4)), dma((2, NB, 4)),
        ],
        compiler_params=pltpu.CompilerParams(
            collective_id=0, has_side_effects=True, vmem_limit_bytes=60 * 1024 * 1024
        ),
    )(signal, delay, fraction, weight)


def solution(mesh):
    return jax.shard_map(
        shards,
        mesh=mesh,
        in_specs=(P("mic", "tm"), P("tm", "mic", None), P("mic", None), P("mic", None)),
        out_specs=P("mic", "tm"),
        check_vma=False,
    )
```

```python
import math

import jax
import jax.numpy as jnp
from jax import lax
from jax.experimental import pallas as pl
from jax.experimental.pallas import tpu as pltpu
from jax.sharding import PartitionSpec as P

MESH = pl.DeviceIdType.MESH
BF, F32, I16 = jnp.bfloat16, jnp.float32, jnp.int16
MICS, FOCUS, HALF, NB, SUB, TIME = 32, 1024, 512, 8, 256, 2048
RING = 8
WIDE = TIME + 128


def series(y, terms):
    r = jnp.full_like(y, terms[-1])
    for c in terms[-2::-1]:
        r = r * y + c
    return r


SIN = [(-1) ** k * math.pi ** (2 * k + 1) / math.factorial(2 * k + 1) for k in range(7)]
COS = [(-1) ** k * math.pi ** (2 * k) / math.factorial(2 * k) for k in range(6)]


def eight_taps(frac, weight):
    low = jnp.minimum(frac, 1.0 - frac)
    scaled = series(low * low, SIN) * low * weight * (1.0 / math.pi)
    quarter = frac * 0.25
    square = quarter * quarter
    s, c = series(square, SIN) * quarter, series(square, COS)
    taps = []
    for r in range(8):
        x = (r - 3.0) - frac
        a = math.pi * (r - 3) / 4.0
        window = 0.5 + (0.5 * math.cos(a)) * c + (0.5 * math.sin(a)) * s
        tap = (scaled if r % 2 == 0 else -scaled) / x * window
        if r in (3, 4):
            tap = jnp.where(x == 0.0, weight, tap)
        taps.append(tap.astype(BF))
    return taps


def tile(mh, fc):
    return pl.ds(mh * 16, 16), pl.ds(fc * 128, 128)


def fill_taps(fw, taps):
    for mh in range(2):
        for fc in range(4):
            rows, cols = tile(mh, fc)
            for p, t in enumerate(eight_taps(fw[0, rows, cols], fw[1, rows, cols])):
                taps[p, rows, cols] = t


def coefficients(taps, delay):
    zero = jnp.zeros((16, 128), BF)
    columns = []
    for fc in range(4):
        parts = []
        for mh in range(2):
            rows, cols = tile(mh, fc)
            t = [taps[p, rows, cols] for p in range(8)]
            d = delay[rows, cols]
            row, column = (d >> I16(3)).astype(BF), (d & I16(7)).astype(BF)
            after = row + BF(1)
            at = [jnp.where(column > BF(q), after, row) for q in range(8)]
            for bit in (4, 2, 1):
                on = (d & I16(bit)).astype(BF) != BF(0)
                t = [jnp.where(on, t[(q - bit) % 8], t[q]) for q in range(8)]
            parts.append((t, at))
        columns.append(
            jnp.concatenate(
                [jnp.where(at[q] == BF(h), t[q], zero) for h in range(8) for q in range(8) for t, at in parts],
                axis=0,
            )
        )
    return jnp.concatenate(columns, axis=1)


def spread(sig, first, blocks, g, hh):
    wide = SUB * blocks + 128
    s = sig[:, pl.ds(pl.multiple_of(first * SUB, 128), wide)].astype(F32)
    g[pl.ds(0, wide), :] = jnp.concatenate([s] + [pltpu.roll(s, wide - k, 1) for k in range(1, 4)], axis=0).T
    rows = SUB * blocks + 48
    for k in range(4):
        hh[pl.ds(0, rows), pl.ds(k * 128, 128)] = g[pl.ds(4 * k, rows), :].astype(BF)


def block_dot(hh, odd, taps, delay):
    lhs = jnp.concatenate([hh[pl.ds(SUB * odd + 16 * k, SUB), :] for k in range(4)], axis=1)
    return jnp.dot(lhs, coefficients(taps, delay), preferred_element_type=F32)


def halves(wide, put):
    lane = lax.broadcasted_iota(jnp.int32, (MICS, 128), 1)
    for i in range(4):
        c0, c1 = wide(2 * i), wide(2 * i + 1)
        put(0, i, jnp.where(lane < 64, c0, pltpu.roll(c1, 64, 1)))
        put(1, i, jnp.where(lane < 64, pltpu.roll(c0, 64, 1), c1))


def kernel(signal, delay, fraction, weight, out,
           sig, psig, raw, dly, pdly, fwraw, fw, pfw, taps, ptaps, g, hh, own, part, sbuf, rbuf,
           lsem, xs, xr, ds_, dr, gs, gr, hs, hr, ss, rs):
    mic, tm = lax.axis_index("mic"), lax.axis_index("tm")
    z, h = mic // 2, lax.rem(mic, 2)
    other = z * 2 + 1 - h
    right = lax.rem(z + 1, RING) * 2 + h
    left = lax.rem(z + RING - 1, RING) * 2 + h
    ntm = lax.axis_size("tm")

    bar = pltpu.get_barrier_semaphore()
    core = lax.rem(tm, 2)
    sibling = tm + 1 - 2 * core
    for peer, at in ((other, tm), (right, tm), (left, tm), (mic, sibling)):
        pl.semaphore_signal(bar, inc=1, device_id={"mic": peer, "tm": at}, device_id_type=MESH)

    @pl.when(tm < ntm - 1)
    def _():
        for peer in (mic, other):
            pl.semaphore_signal(bar, inc=1, device_id={"mic": peer, "tm": tm + 1}, device_id_type=MESH)

    loads = [
        pltpu.make_async_copy(fraction, fwraw.at[0], lsem.at[0]),
        pltpu.make_async_copy(weight, fwraw.at[1], lsem.at[1]),
        pltpu.make_async_copy(delay.at[0], raw.at[0], lsem.at[2]),
        pltpu.make_async_copy(signal, sig.at[:, pl.ds(0, TIME)], lsem.at[3]),
        pltpu.make_async_copy(delay.at[pl.ds(1, NB - 1)], raw.at[pl.ds(1, NB - 1)], lsem.at[4]),
    ]
    for c in loads:
        c.start()

    @pl.when(tm == ntm - 1)
    def _():
        sig[:, pl.ds(TIME, 128)] = jnp.zeros((MICS, 128), BF)
        psig[:, pl.ds(TIME, 128)] = jnp.zeros((MICS, 128), BF)

    def remote(src, dst, send, recv, **to):
        return pltpu.make_async_remote_copy(src, dst, send, recv, device_id={"mic": mic, "tm": tm, **to}, device_id_type=MESH)

    def send_fw():
        return remote(fw.at[1 - h, core], pfw.at[core], gs.at[0], gr.at[0], mic=other)

    def share_fw():
        return remote(pfw.at[core], pfw.at[core], gs.at[1], gr.at[1], tm=sibling)

    def send_delay(b):
        return remote(dly.at[1 - h, b], pdly.at[b], ds_.at[b], dr.at[b], mic=other)

    def send_piece(c):
        cols = pl.ds(pl.multiple_of(c * SUB, 128), SUB)
        return remote(sig.at[:, cols], psig.at[:, cols], xs.at[c], xr.at[c], mic=other)

    def send_halo(k):
        dst = (sig, psig)[k]
        peer = (mic, other)[k]
        return remote(sig.at[:, pl.ds(0, 128)], dst.at[:, pl.ds(TIME, 128)], hs.at[k], hr.at[k], mic=peer, tm=tm - 1)

    def wait_halo(k):
        dst = (sig, psig)[k]
        remote(sig.at[:, pl.ds(0, 128)], dst.at[:, pl.ds(TIME, 128)], hs.at[k], hr.at[k]).wait_recv()

    loads[0].wait()
    loads[1].wait()
    for k in range(2):
        def put(half, i, v, k=k):
            fw[half, k, :, pl.ds(i * 128, 128)] = v
        halves(lambda i, k=k: fwraw[k, :, pl.ds(i * 128, 128)], put)

    def compact(b):
        def put(half, i, v):
            dly[half, b, :, pl.ds(i * 128, 128)] = v.astype(I16)
        halves(lambda i: raw[b, :, pl.ds(i * 128, 128)], put)

    loads[2].wait()
    compact(0)
    loads[3].wait()

    @pl.when(tm > 0)
    def _():
        pl.semaphore_wait(bar, 6)

    @pl.when(tm == 0)
    def _():
        pl.semaphore_wait(bar, 4)

    send_fw().start()
    send_piece(0).start()
    send_piece(1).start()
    send_delay(0).start()
    loads[4].wait()

    def pass_on(b):
        if b < NB - 1:
            send_piece(b + 1).start()
        compact(b)
        send_delay(b).start()

    pass_on(1)
    pass_on(2)

    @pl.when(tm > 0)
    def _():
        send_halo(0).start()
        send_halo(1).start()

    fill_taps(fw.at[h], taps)

    def half(pair):
        spread(sig, 2 * pair, 2, g, hh)
        for odd in range(2):
            own[2 * pair + odd] = block_dot(hh, odd, taps, dly.at[h, 2 * pair + odd])

    half(0)
    for b in range(3, NB):
        pass_on(b)
    send_fw().wait_recv()
    share_fw().start()
    half(1)
    share_fw().wait_recv()
    fill_taps(pfw, ptaps)
    send_piece(0).wait_recv()

    lane = lax.broadcasted_iota(jnp.int32, (128, 128), 1)

    def message(b, way, hop):
        peer = (right, left)[way]
        return remote(sbuf.at[way, b, hop], rbuf.at[way, b, hop], ss.at[way, b, hop], rs.at[way, b, hop], mic=peer)

    def length(odd, way):
        return 4 if odd == way else 3

    def hop(pair, odd, k):
        for way in range(2):
            steps = length(odd, way)
            if k >= steps:
                continue
            b = 2 * pair + odd
            ahead = steps - k
            dest = lax.rem(z + (ahead if way == 0 else RING - ahead), RING)
            total = part[b, dest]
            if k > 0:
                message(b, way, k - 1).wait_recv()
                total = total + rbuf[way, b, k - 1].astype(F32)
            sbuf[way, b, k] = total.astype(BF)
            message(b, way, k).start()

    def finish(pair):
        for odd in range(2):
            b = 2 * pair + odd
            total = part[b, z]
            for way in range(2):
                last = length(odd, way) - 1
                message(b, way, last).wait_recv()
                total = total + rbuf[way, b, last].astype(F32)
            flat = total.T
            start = pl.multiple_of(b * SUB, 128)
            out[:, pl.ds(start, 128)] = flat[0:64, :]
            out[:, pl.ds(pl.multiple_of(start + 128, 128), 128)] = flat[64:128, :]

    def form(first, blocks):
        for odd in range(blocks):
            b = first + odd
            r = own[b] + block_dot(hh, odd, ptaps, pdly.at[b])
            for i in range(4):
                top, bottom = r[0:128, i * 128 : i * 128 + 128], r[128:256, i * 128 : i * 128 + 128]
                part[b, 2 * i] = jnp.where(lane < 64, top, pltpu.roll(bottom, 64, 1))
                part[b, 2 * i + 1] = jnp.where(lane < 64, pltpu.roll(top, 64, 1), bottom)

    last = NB // 2 - 1

    @pl.loop(0, 2)
    def _(b):
        send_piece(b + 1).wait_recv()
        spread(psig, b, 1, g, hh)
        send_delay(b).wait_recv()
        form(b, 1)

        for odd in range(2):
            @pl.when(b == odd)
            def _(odd=odd):
                hop(0, odd, 0)

    @pl.loop(1, NB // 2)
    def _(i):
        @pl.when((i == last) & (tm < ntm - 1))
        def _():
            wait_halo(0)

        @pl.when(i >= 2)
        def _():
            half(i)
            for odd in range(2):
                hop(i - 2, odd, 1)

        send_delay(2 * i).wait_recv()
        send_piece(2 * i + 1).wait_recv()
        send_delay(2 * i + 1).wait_recv()

        @pl.when(i < last)
        def _():
            send_piece(2 * i + 2).wait_recv()

        @pl.when((i == last) & (tm < ntm - 1))
        def _():
            wait_halo(1)

        spread(psig, 2 * i, 2, g, hh)
        form(2 * i, 2)
        for odd in range(2):
            hop(i, odd, 0)
    for odd in range(2):
        hop(last - 1, odd, 1)
    for odd in range(2):
        hop(0, odd, 2)
    for odd in range(2):
        hop(last, odd, 1)

    @pl.loop(1, NB // 2)
    def _(i):
        for odd in range(2):
            hop(i, odd, 2)

    @pl.loop(0, NB // 2)
    def _(i):
        for odd in range(2):
            hop(i, odd, 3)

    @pl.loop(0, NB // 2)
    def _(i):
        finish(i)

    send_fw().wait_send()
    share_fw().wait_send()

    @pl.loop(0, NB)
    def _(b):
        send_delay(b).wait_send()
        send_piece(b).wait_send()

    @pl.when(tm > 0)
    def _():
        send_halo(0).wait_send()
        send_halo(1).wait_send()

    @pl.loop(0, NB // 2)
    def _(i):
        for odd in range(2):
            for way in range(2):
                for k in range(length(odd, way)):
                    message(2 * i + odd, way, k).wait_send()


def shards(signal, delay, fraction, weight):
    dma = pltpu.SemaphoreType.DMA
    return pl.pallas_call(
        kernel,
        out_shape=pltpu.VMEM((FOCUS // 16, TIME), F32),
        in_specs=[pl.BlockSpec(memory_space=pltpu.HBM)] * 4,
        out_specs=pl.BlockSpec(memory_space=pltpu.VMEM),
        scratch_shapes=[
            pltpu.VMEM((MICS, WIDE), BF),
            pltpu.VMEM((MICS, WIDE), BF),
            pltpu.VMEM((NB, MICS, FOCUS), jnp.int32),
            pltpu.VMEM((2, NB, MICS, HALF), I16),
            pltpu.VMEM((NB, MICS, HALF), I16),
            pltpu.VMEM((2, MICS, FOCUS), F32),
            pltpu.VMEM((2, 2, MICS, HALF), F32),
            pltpu.VMEM((2, MICS, HALF), F32),
            pltpu.VMEM((8, MICS, HALF), BF),
            pltpu.VMEM((8, MICS, HALF), BF),
            pltpu.VMEM((640, 128), F32),
            pltpu.VMEM((2 * SUB + 48, 512), BF),
            pltpu.VMEM((NB, SUB, HALF), F32),
            pltpu.VMEM((NB, RING, 128, 128), F32),
            pltpu.VMEM((2, NB, 4, 128, 128), BF),
            pltpu.VMEM((2, NB, 4, 128, 128), BF),
            dma((5,)),
            dma((NB,)), dma((NB,)),
            dma((NB,)), dma((NB,)),
            dma((2,)), dma((2,)),
            dma((2,)), dma((2,)),
            dma((2, NB, 4)), dma((2, NB, 4)),
        ],
        compiler_params=pltpu.CompilerParams(
            collective_id=0, has_side_effects=True, vmem_limit_bytes=40 * 1024 * 1024
        ),
    )(*(pltpu.with_memory_space_constraint(x, pltpu.HBM) for x in (signal, delay, fraction, weight)))


def solution(mesh):
    return jax.shard_map(
        shards,
        mesh=mesh,
        in_specs=(P("mic", "tm"), P("tm", "mic", None), P("mic", None), P("mic", None)),
        out_specs=P("mic", "tm"),
        check_vma=False,
    )
```

```python
import math

import jax
import jax.numpy as jnp
from jax import lax
from jax.experimental import pallas as pl
from jax.experimental.pallas import tpu as pltpu
from jax.sharding import PartitionSpec as P

MESH = pl.DeviceIdType.MESH
BF, F32, I16 = jnp.bfloat16, jnp.float32, jnp.int16
MICS, FOCUS, HALF, NB, SUB, TIME = 32, 1024, 512, 8, 256, 2048
RING = 8
WIDE = TIME + 128


def series(y, terms):
    r = jnp.full_like(y, terms[-1])
    for c in terms[-2::-1]:
        r = r * y + c
    return r


SIN = [(-1) ** k * math.pi ** (2 * k + 1) / math.factorial(2 * k + 1) for k in range(7)]
COS = [(-1) ** k * math.pi ** (2 * k) / math.factorial(2 * k) for k in range(6)]


def eight_taps(frac, weight):
    low = jnp.minimum(frac, 1.0 - frac)
    scaled = series(low * low, SIN) * low * weight * (1.0 / math.pi)
    quarter = frac * 0.25
    square = quarter * quarter
    s, c = series(square, SIN) * quarter, series(square, COS)
    taps = []
    for r in range(8):
        x = (r - 3.0) - frac
        a = math.pi * (r - 3) / 4.0
        window = 0.5 + (0.5 * math.cos(a)) * c + (0.5 * math.sin(a)) * s
        tap = (scaled if r % 2 == 0 else -scaled) / x * window
        if r in (3, 4):
            tap = jnp.where(x == 0.0, weight, tap)
        taps.append(tap.astype(BF))
    return taps


def tile(mh, fc):
    return pl.ds(mh * 16, 16), pl.ds(fc * 128, 128)


def fill_taps(fw, taps):
    for mh in range(2):
        for fc in range(4):
            rows, cols = tile(mh, fc)
            for p, t in enumerate(eight_taps(fw[0, rows, cols], fw[1, rows, cols])):
                taps[p, rows, cols] = t


def coefficients(taps, delay):
    zero = jnp.zeros((16, 128), BF)
    columns = []
    for fc in range(4):
        parts = []
        for mh in range(2):
            rows, cols = tile(mh, fc)
            t = [taps[p, rows, cols] for p in range(8)]
            d = delay[rows, cols]
            row, column = (d >> I16(3)).astype(BF), (d & I16(7)).astype(BF)
            after = row + BF(1)
            at = [jnp.where(column > BF(q), after, row) for q in range(8)]
            for bit in (4, 2, 1):
                on = (d & I16(bit)).astype(BF) != BF(0)
                t = [jnp.where(on, t[(q - bit) % 8], t[q]) for q in range(8)]
            parts.append((t, at))
        columns.append(
            jnp.concatenate(
                [jnp.where(at[q] == BF(h), t[q], zero) for h in range(8) for q in range(8) for t, at in parts],
                axis=0,
            )
        )
    return jnp.concatenate(columns, axis=1)


def spread(sig, first, blocks, g, hh):
    wide = SUB * blocks + 128
    s = sig[:, pl.ds(pl.multiple_of(first * SUB, 128), wide)].astype(F32)
    g[pl.ds(0, wide), :] = jnp.concatenate([s] + [pltpu.roll(s, wide - k, 1) for k in range(1, 4)], axis=0).T
    rows = SUB * blocks + 48
    for k in range(4):
        hh[pl.ds(0, rows), pl.ds(k * 128, 128)] = g[pl.ds(4 * k, rows), :].astype(BF)


def block_dot(hh, odd, taps, delay):
    lhs = jnp.concatenate([hh[pl.ds(SUB * odd + 16 * k, SUB), :] for k in range(4)], axis=1)
    return jnp.dot(lhs, coefficients(taps, delay), preferred_element_type=F32)


def halves(wide, put):
    lane = lax.broadcasted_iota(jnp.int32, (MICS, 128), 1)
    for i in range(4):
        c0, c1 = wide(2 * i), wide(2 * i + 1)
        put(0, i, jnp.where(lane < 64, c0, pltpu.roll(c1, 64, 1)))
        put(1, i, jnp.where(lane < 64, pltpu.roll(c0, 64, 1), c1))


def kernel(signal, delay, fraction, weight, out,
           sig, psig, raw, dly, pdly, fwraw, fw, pfw, taps, ptaps, g, hh, own, part, sbuf, rbuf,
           lsem, xs, xr, ds_, dr, gs, gr, hs, hr, ss, rs):
    mic, tm = lax.axis_index("mic"), lax.axis_index("tm")
    z, h = mic // 2, lax.rem(mic, 2)
    other = z * 2 + 1 - h
    right = lax.rem(z + 1, RING) * 2 + h
    left = lax.rem(z + RING - 1, RING) * 2 + h
    ntm = lax.axis_size("tm")

    bar = pltpu.get_barrier_semaphore()
    core = lax.rem(tm, 2)
    sibling = tm + 1 - 2 * core
    for peer, at in ((other, tm), (right, tm), (left, tm), (mic, sibling)):
        pl.semaphore_signal(bar, inc=1, device_id={"mic": peer, "tm": at}, device_id_type=MESH)

    @pl.when(tm < ntm - 1)
    def _():
        for peer in (mic, other):
            pl.semaphore_signal(bar, inc=1, device_id={"mic": peer, "tm": tm + 1}, device_id_type=MESH)

    loads = [
        pltpu.make_async_copy(fraction, fwraw.at[0], lsem.at[0]),
        pltpu.make_async_copy(weight, fwraw.at[1], lsem.at[1]),
        pltpu.make_async_copy(delay.at[0], raw.at[0], lsem.at[2]),
        pltpu.make_async_copy(signal, sig.at[:, pl.ds(0, TIME)], lsem.at[3]),
        pltpu.make_async_copy(delay.at[pl.ds(1, NB - 1)], raw.at[pl.ds(1, NB - 1)], lsem.at[4]),
    ]
    for k in (3, 0, 1, 2, 4):
        loads[k].start()

    @pl.when(tm == ntm - 1)
    def _():
        sig[:, pl.ds(TIME, 128)] = jnp.zeros((MICS, 128), BF)
        psig[:, pl.ds(TIME, 128)] = jnp.zeros((MICS, 128), BF)

    def remote(src, dst, send, recv, **to):
        return pltpu.make_async_remote_copy(src, dst, send, recv, device_id={"mic": mic, "tm": tm, **to}, device_id_type=MESH)

    def send_fw():
        return remote(fw.at[1 - h, core], pfw.at[core], gs.at[0], gr.at[0], mic=other)

    def share_fw():
        return remote(pfw.at[core], pfw.at[core], gs.at[1], gr.at[1], tm=sibling)

    def send_delay(b):
        return remote(dly.at[1 - h, b], pdly.at[b], ds_.at[b], dr.at[b], mic=other)

    def send_piece(c):
        cols = pl.ds(pl.multiple_of(c * SUB, 128), SUB)
        return remote(sig.at[:, cols], psig.at[:, cols], xs.at[c], xr.at[c], mic=other)

    def send_halo(k):
        dst = (sig, psig)[k]
        peer = (mic, other)[k]
        return remote(sig.at[:, pl.ds(0, 128)], dst.at[:, pl.ds(TIME, 128)], hs.at[k], hr.at[k], mic=peer, tm=tm - 1)

    def wait_halo(k):
        dst = (sig, psig)[k]
        remote(sig.at[:, pl.ds(0, 128)], dst.at[:, pl.ds(TIME, 128)], hs.at[k], hr.at[k]).wait_recv()

    loads[3].wait()

    @pl.when(tm > 0)
    def _():
        pl.semaphore_wait(bar, 6)

    @pl.when(tm == 0)
    def _():
        pl.semaphore_wait(bar, 4)

    send_piece(0).start()
    send_piece(1).start()
    loads[0].wait()
    loads[1].wait()
    for k in range(2):
        def put(half, i, v, k=k):
            fw[half, k, :, pl.ds(i * 128, 128)] = v
        halves(lambda i, k=k: fwraw[k, :, pl.ds(i * 128, 128)], put)
    send_fw().start()

    def compact(b):
        def put(half, i, v):
            dly[half, b, :, pl.ds(i * 128, 128)] = v.astype(I16)
        halves(lambda i: raw[b, :, pl.ds(i * 128, 128)], put)

    loads[2].wait()
    compact(0)
    send_delay(0).start()
    loads[4].wait()

    def pass_on(b):
        if b < NB - 1:
            send_piece(b + 1).start()
        compact(b)
        send_delay(b).start()

    pass_on(1)
    pass_on(2)

    @pl.when(tm > 0)
    def _():
        send_halo(0).start()
        send_halo(1).start()

    fill_taps(fw.at[h], taps)

    def half(pair):
        spread(sig, 2 * pair, 2, g, hh)
        for odd in range(2):
            own[2 * pair + odd] = block_dot(hh, odd, taps, dly.at[h, 2 * pair + odd])

    half(0)
    for b in range(3, NB):
        pass_on(b)
    send_fw().wait_recv()
    share_fw().start()
    half(1)
    share_fw().wait_recv()
    fill_taps(pfw, ptaps)
    send_piece(0).wait_recv()

    lane = lax.broadcasted_iota(jnp.int32, (128, 128), 1)

    def message(b, way, hop):
        peer = (right, left)[way]
        return remote(sbuf.at[way, b, hop], rbuf.at[way, b, hop], ss.at[way, b, hop], rs.at[way, b, hop], mic=peer)

    def length(odd, way):
        return 4 if odd == way else 3

    def hop(pair, odd, k):
        for way in range(2):
            steps = length(odd, way)
            if k >= steps:
                continue
            b = 2 * pair + odd
            ahead = steps - k
            dest = lax.rem(z + (ahead if way == 0 else RING - ahead), RING)
            total = part[b, dest]
            if k > 0:
                message(b, way, k - 1).wait_recv()
                total = total + rbuf[way, b, k - 1].astype(F32)
            sbuf[way, b, k] = total.astype(BF)
            message(b, way, k).start()

    def finish(pair):
        for odd in range(2):
            b = 2 * pair + odd
            total = part[b, z]
            for way in range(2):
                last = length(odd, way) - 1
                message(b, way, last).wait_recv()
                total = total + rbuf[way, b, last].astype(F32)
            flat = total.T
            start = pl.multiple_of(b * SUB, 128)
            out[:, pl.ds(start, 128)] = flat[0:64, :]
            out[:, pl.ds(pl.multiple_of(start + 128, 128), 128)] = flat[64:128, :]

    def form(first, blocks):
        for odd in range(blocks):
            b = first + odd
            r = own[b] + block_dot(hh, odd, ptaps, pdly.at[b])
            for i in range(4):
                top, bottom = r[0:128, i * 128 : i * 128 + 128], r[128:256, i * 128 : i * 128 + 128]
                part[b, 2 * i] = jnp.where(lane < 64, top, pltpu.roll(bottom, 64, 1))
                part[b, 2 * i + 1] = jnp.where(lane < 64, pltpu.roll(top, 64, 1), bottom)

    last = NB // 2 - 1

    @pl.loop(0, 2)
    def _(b):
        send_piece(b + 1).wait_recv()
        spread(psig, b, 1, g, hh)
        send_delay(b).wait_recv()
        form(b, 1)

        for odd in range(2):
            @pl.when(b == odd)
            def _(odd=odd):
                hop(0, odd, 0)

    @pl.loop(1, NB // 2)
    def _(i):
        @pl.when((i == last) & (tm < ntm - 1))
        def _():
            wait_halo(0)

        @pl.when(i >= 2)
        def _():
            half(i)

        @pl.when(i == 2)
        def _():
            for odd in range(2):
                hop(0, odd, 1)

        @pl.when(i == 3)
        def _():
            for odd in range(2):
                hop(0, odd, 2)

        send_delay(2 * i).wait_recv()
        send_piece(2 * i + 1).wait_recv()
        send_delay(2 * i + 1).wait_recv()

        @pl.when(i < last)
        def _():
            send_piece(2 * i + 2).wait_recv()

        @pl.when((i == last) & (tm < ntm - 1))
        def _():
            wait_halo(1)

        spread(psig, 2 * i, 2, g, hh)
        form(2 * i, 2)
        for odd in range(2):
            hop(i, odd, 0)

        @pl.when(i == 2)
        def _():
            for odd in range(2):
                hop(1, odd, 1)

    for odd in range(2):
        hop(2, odd, 1)
    for odd in range(2):
        hop(1, odd, 2)
    for odd in range(2):
        hop(3, odd, 1)
    for odd in range(2):
        hop(2, odd, 2)
    for odd in range(2):
        hop(3, odd, 2)

    @pl.loop(0, NB // 2)
    def _(i):
        for odd in range(2):
            hop(i, odd, 3)

    @pl.loop(0, last)
    def _(i):
        finish(i)

    send_fw().wait_send()
    share_fw().wait_send()

    @pl.loop(0, NB)
    def _(b):
        send_delay(b).wait_send()
        send_piece(b).wait_send()

    @pl.when(tm > 0)
    def _():
        send_halo(0).wait_send()
        send_halo(1).wait_send()

    @pl.loop(0, NB // 2)
    def _(i):
        for odd in range(2):
            for way in range(2):
                for k in range(length(odd, way)):
                    message(2 * i + odd, way, k).wait_send()

    finish(last)


def shards(signal, delay, fraction, weight):
    dma = pltpu.SemaphoreType.DMA
    return pl.pallas_call(
        kernel,
        out_shape=pltpu.VMEM((FOCUS // 16, TIME), F32),
        in_specs=[pl.BlockSpec(memory_space=pltpu.HBM)] * 4,
        out_specs=pl.BlockSpec(memory_space=pltpu.VMEM),
        scratch_shapes=[
            pltpu.VMEM((MICS, WIDE), BF),
            pltpu.VMEM((MICS, WIDE), BF),
            pltpu.VMEM((NB, MICS, FOCUS), jnp.int32),
            pltpu.VMEM((2, NB, MICS, HALF), I16),
            pltpu.VMEM((NB, MICS, HALF), I16),
            pltpu.VMEM((2, MICS, FOCUS), F32),
            pltpu.VMEM((2, 2, MICS, HALF), F32),
            pltpu.VMEM((2, MICS, HALF), F32),
            pltpu.VMEM((8, MICS, HALF), BF),
            pltpu.VMEM((8, MICS, HALF), BF),
            pltpu.VMEM((640, 128), F32),
            pltpu.VMEM((2 * SUB + 48, 512), BF),
            pltpu.VMEM((NB, SUB, HALF), F32),
            pltpu.VMEM((NB, RING, 128, 128), F32),
            pltpu.VMEM((2, NB, 4, 128, 128), BF),
            pltpu.VMEM((2, NB, 4, 128, 128), BF),
            dma((5,)),
            dma((NB,)), dma((NB,)),
            dma((NB,)), dma((NB,)),
            dma((2,)), dma((2,)),
            dma((2,)), dma((2,)),
            dma((2, NB, 4)), dma((2, NB, 4)),
        ],
        compiler_params=pltpu.CompilerParams(
            collective_id=0, has_side_effects=True, vmem_limit_bytes=40 * 1024 * 1024
        ),
    )(*(pltpu.with_memory_space_constraint(x, pltpu.HBM) for x in (signal, delay, fraction, weight)))


def solution(mesh):
    return jax.shard_map(
        shards,
        mesh=mesh,
        in_specs=(P("mic", "tm"), P("tm", "mic", None), P("mic", None), P("mic", None)),
        out_specs=P("mic", "tm"),
        check_vma=False,
    )
```

```python
import math

import jax
import jax.numpy as jnp
from jax import lax
from jax.experimental import pallas as pl
from jax.experimental.pallas import tpu as pltpu
from jax.sharding import PartitionSpec as P

MESH = pl.DeviceIdType.MESH
BF, F32, I16 = jnp.bfloat16, jnp.float32, jnp.int16
MICS, FOCUS, HALF, NB, SUB, TIME = 32, 1024, 512, 8, 256, 2048
RING = 8
WIDE = TIME + 128


def series(y, terms):
    r = jnp.full_like(y, terms[-1])
    for c in terms[-2::-1]:
        r = r * y + c
    return r


SIN = [(-1) ** k * math.pi ** (2 * k + 1) / math.factorial(2 * k + 1) for k in range(7)]
COS = [(-1) ** k * math.pi ** (2 * k) / math.factorial(2 * k) for k in range(6)]


def eight_taps(frac, weight):
    low = jnp.minimum(frac, 1.0 - frac)
    scaled = series(low * low, SIN) * low * weight * (1.0 / math.pi)
    quarter = frac * 0.25
    square = quarter * quarter
    s, c = series(square, SIN) * quarter, series(square, COS)
    taps = []
    for r in range(8):
        x = (r - 3.0) - frac
        a = math.pi * (r - 3) / 4.0
        window = 0.5 + (0.5 * math.cos(a)) * c + (0.5 * math.sin(a)) * s
        tap = (scaled if r % 2 == 0 else -scaled) / x * window
        if r in (3, 4):
            tap = jnp.where(x == 0.0, weight, tap)
        taps.append(tap.astype(BF))
    return taps


def tile(mh, fc):
    return pl.ds(mh * 16, 16), pl.ds(fc * 128, 128)


def fill_taps(fw, taps):
    for mh in range(2):
        for fc in range(4):
            rows, cols = tile(mh, fc)
            for p, t in enumerate(eight_taps(fw[0, rows, cols], fw[1, rows, cols])):
                taps[p, rows, cols] = t


def coefficients(taps, delay):
    zero = jnp.zeros((16, 128), BF)
    columns = []
    for fc in range(4):
        parts = []
        for mh in range(2):
            rows, cols = tile(mh, fc)
            t = [taps[p, rows, cols] for p in range(8)]
            d = delay[rows, cols]
            row, column = (d >> I16(3)).astype(BF), (d & I16(7)).astype(BF)
            after = row + BF(1)
            at = [jnp.where(column > BF(q), after, row) for q in range(8)]
            for bit in (4, 2, 1):
                on = (d & I16(bit)).astype(BF) != BF(0)
                t = [jnp.where(on, t[(q - bit) % 8], t[q]) for q in range(8)]
            parts.append((t, at))
        columns.append(
            jnp.concatenate(
                [jnp.where(at[q] == BF(h), t[q], zero) for h in range(8) for q in range(8) for t, at in parts],
                axis=0,
            )
        )
    return jnp.concatenate(columns, axis=1)


def spread(sig, first, blocks, g, hh):
    wide = SUB * blocks + 128
    s = sig[:, pl.ds(pl.multiple_of(first * SUB, 128), wide)].astype(F32)
    g[pl.ds(0, wide), :] = jnp.concatenate([s] + [pltpu.roll(s, wide - k, 1) for k in range(1, 4)], axis=0).T
    rows = SUB * blocks + 48
    for k in range(4):
        hh[pl.ds(0, rows), pl.ds(k * 128, 128)] = g[pl.ds(4 * k, rows), :].astype(BF)


def block_dot(hh, odd, taps, delay):
    lhs = jnp.concatenate([hh[pl.ds(SUB * odd + 16 * k, SUB), :] for k in range(4)], axis=1)
    return jnp.dot(lhs, coefficients(taps, delay), preferred_element_type=F32)


def halves(wide, put):
    lane = lax.broadcasted_iota(jnp.int32, (MICS, 128), 1)
    for i in range(4):
        c0, c1 = wide(2 * i), wide(2 * i + 1)
        put(0, i, jnp.where(lane < 64, c0, pltpu.roll(c1, 64, 1)))
        put(1, i, jnp.where(lane < 64, pltpu.roll(c0, 64, 1), c1))


def kernel(signal, delay, fraction, weight, out,
           sig, psig, raw, dly, pdly, fwraw, fw, pfw, taps, ptaps, g, hh, own, part, sbuf, rbuf,
           lsem, xs, xr, ds_, dr, gs, gr, hs, hr, ss, rs):
    mic, tm = lax.axis_index("mic"), lax.axis_index("tm")
    z, h = mic // 2, lax.rem(mic, 2)
    other = z * 2 + 1 - h
    right = lax.rem(z + 1, RING) * 2 + h
    left = lax.rem(z + RING - 1, RING) * 2 + h
    ntm = lax.axis_size("tm")

    bar = pltpu.get_barrier_semaphore()
    core = lax.rem(tm, 2)
    sibling = tm + 1 - 2 * core
    for peer, at in ((other, tm), (right, tm), (left, tm), (mic, sibling)):
        pl.semaphore_signal(bar, inc=1, device_id={"mic": peer, "tm": at}, device_id_type=MESH)

    @pl.when(tm < ntm - 1)
    def _():
        for peer in (mic, other):
            pl.semaphore_signal(bar, inc=1, device_id={"mic": peer, "tm": tm + 1}, device_id_type=MESH)

    loads = [
        pltpu.make_async_copy(fraction, fwraw.at[0], lsem.at[0]),
        pltpu.make_async_copy(weight, fwraw.at[1], lsem.at[1]),
        pltpu.make_async_copy(delay.at[0], raw.at[0], lsem.at[2]),
        pltpu.make_async_copy(signal, sig.at[:, pl.ds(0, TIME)], lsem.at[3]),
        pltpu.make_async_copy(delay.at[pl.ds(1, NB - 1)], raw.at[pl.ds(1, NB - 1)], lsem.at[4]),
    ]
    for k in (3, 0, 1, 2, 4):
        loads[k].start()

    @pl.when(tm == ntm - 1)
    def _():
        sig[:, pl.ds(TIME, 128)] = jnp.zeros((MICS, 128), BF)
        psig[:, pl.ds(TIME, 128)] = jnp.zeros((MICS, 128), BF)

    def remote(src, dst, send, recv, **to):
        return pltpu.make_async_remote_copy(src, dst, send, recv, device_id={"mic": mic, "tm": tm, **to}, device_id_type=MESH)

    def send_fw():
        return remote(fw.at[1 - h, core], pfw.at[core], gs.at[0], gr.at[0], mic=other)

    def share_fw():
        return remote(pfw.at[core], pfw.at[core], gs.at[1], gr.at[1], tm=sibling)

    def send_delay(b):
        return remote(dly.at[1 - h, b], pdly.at[b], ds_.at[b], dr.at[b], mic=other)

    def send_piece(c):
        cols = pl.ds(pl.multiple_of(c * SUB, 128), SUB)
        return remote(sig.at[:, cols], psig.at[:, cols], xs.at[c], xr.at[c], mic=other)

    def send_halo(k):
        dst = (sig, psig)[k]
        peer = (mic, other)[k]
        return remote(sig.at[:, pl.ds(0, 128)], dst.at[:, pl.ds(TIME, 128)], hs.at[k], hr.at[k], mic=peer, tm=tm - 1)

    def wait_halo(k):
        dst = (sig, psig)[k]
        remote(sig.at[:, pl.ds(0, 128)], dst.at[:, pl.ds(TIME, 128)], hs.at[k], hr.at[k]).wait_recv()

    loads[3].wait()

    @pl.when(tm > 0)
    def _():
        pl.semaphore_wait(bar, 6)

    @pl.when(tm == 0)
    def _():
        pl.semaphore_wait(bar, 4)

    send_piece(0).start()
    send_piece(1).start()
    loads[0].wait()
    loads[1].wait()
    for k in (core, 1 - core):
        def put(half, i, v, k=k):
            fw[half, k, :, pl.ds(i * 128, 128)] = v
        halves(lambda i, k=k: fwraw[k, :, pl.ds(i * 128, 128)], put)
        if k is core:
            send_fw().start()

    def compact(b):
        def put(half, i, v):
            dly[half, b, :, pl.ds(i * 128, 128)] = v.astype(I16)
        halves(lambda i: raw[b, :, pl.ds(i * 128, 128)], put)

    loads[2].wait()
    compact(0)
    send_delay(0).start()
    loads[4].wait()

    def pass_on(b):
        if b < NB - 1:
            send_piece(b + 1).start()
        compact(b)
        send_delay(b).start()

    pass_on(1)
    pass_on(2)

    @pl.when(tm > 0)
    def _():
        send_halo(0).start()
        send_halo(1).start()

    fill_taps(fw.at[h], taps)

    def half(pair):
        spread(sig, 2 * pair, 2, g, hh)
        for odd in range(2):
            own[2 * pair + odd] = block_dot(hh, odd, taps, dly.at[h, 2 * pair + odd])

    half(0)
    for b in range(3, NB):
        pass_on(b)
    send_fw().wait_recv()
    share_fw().start()
    half(1)
    share_fw().wait_recv()
    fill_taps(pfw, ptaps)
    send_piece(0).wait_recv()

    lane = lax.broadcasted_iota(jnp.int32, (128, 128), 1)

    def message(b, way, hop):
        peer = (right, left)[way]
        return remote(sbuf.at[way, b, hop], rbuf.at[way, b, hop], ss.at[way, b, hop], rs.at[way, b, hop], mic=peer)

    def length(odd, way):
        return 4 if odd == way else 3

    def hop(pair, odd, k):
        for way in range(2):
            steps = length(odd, way)
            if k >= steps:
                continue
            b = 2 * pair + odd
            ahead = steps - k
            dest = lax.rem(z + (ahead if way == 0 else RING - ahead), RING)
            total = part[b, dest]
            if k > 0:
                message(b, way, k - 1).wait_recv()
                total = total + rbuf[way, b, k - 1].astype(F32)
            sbuf[way, b, k] = total.astype(BF)
            message(b, way, k).start()

    def finish(pair):
        for odd in range(2):
            b = 2 * pair + odd
            total = part[b, z]
            for way in range(2):
                last = length(odd, way) - 1
                message(b, way, last).wait_recv()
                total = total + rbuf[way, b, last].astype(F32)
            flat = total.T
            start = pl.multiple_of(b * SUB, 128)
            out[:, pl.ds(start, 128)] = flat[0:64, :]
            out[:, pl.ds(pl.multiple_of(start + 128, 128), 128)] = flat[64:128, :]

    def form(first, blocks):
        for odd in range(blocks):
            b = first + odd
            r = own[b] + block_dot(hh, odd, ptaps, pdly.at[b])
            for i in range(4):
                top, bottom = r[0:128, i * 128 : i * 128 + 128], r[128:256, i * 128 : i * 128 + 128]
                part[b, 2 * i] = jnp.where(lane < 64, top, pltpu.roll(bottom, 64, 1))
                part[b, 2 * i + 1] = jnp.where(lane < 64, pltpu.roll(top, 64, 1), bottom)

    last = NB // 2 - 1

    @pl.loop(0, 2)
    def _(b):
        send_piece(b + 1).wait_recv()
        spread(psig, b, 1, g, hh)
        send_delay(b).wait_recv()
        form(b, 1)

        for odd in range(2):
            @pl.when(b == odd)
            def _(odd=odd):
                hop(0, odd, 0)

    @pl.loop(1, NB // 2)
    def _(i):
        @pl.when((i == last) & (tm < ntm - 1))
        def _():
            wait_halo(0)

        @pl.when(i >= 2)
        def _():
            half(i)

        @pl.when(i == 2)
        def _():
            for odd in range(2):
                hop(0, odd, 1)

        @pl.when(i == 3)
        def _():
            for odd in range(2):
                hop(0, odd, 2)

        send_delay(2 * i).wait_recv()
        send_piece(2 * i + 1).wait_recv()
        send_delay(2 * i + 1).wait_recv()

        @pl.when(i < last)
        def _():
            send_piece(2 * i + 2).wait_recv()

        @pl.when((i == last) & (tm < ntm - 1))
        def _():
            wait_halo(1)

        spread(psig, 2 * i, 2, g, hh)
        form(2 * i, 2)
        for odd in range(2):
            hop(i, odd, 0)

        @pl.when(i == 2)
        def _():
            for odd in range(2):
                hop(1, odd, 1)

    for odd in range(2):
        hop(2, odd, 1)
    for odd in range(2):
        hop(1, odd, 2)
    for odd in range(2):
        hop(3, odd, 1)
    for odd in range(2):
        hop(2, odd, 2)
    for odd in range(2):
        hop(3, odd, 2)

    @pl.loop(0, NB // 2)
    def _(i):
        for odd in range(2):
            hop(i, odd, 3)

    @pl.loop(0, last)
    def _(i):
        finish(i)

    send_fw().wait_send()
    share_fw().wait_send()

    @pl.loop(0, NB)
    def _(b):
        send_delay(b).wait_send()
        send_piece(b).wait_send()

    @pl.when(tm > 0)
    def _():
        send_halo(0).wait_send()
        send_halo(1).wait_send()

    @pl.loop(0, NB // 2)
    def _(i):
        for odd in range(2):
            for way in range(2):
                for k in range(length(odd, way)):
                    message(2 * i + odd, way, k).wait_send()

    finish(last)


def shards(signal, delay, fraction, weight):
    dma = pltpu.SemaphoreType.DMA
    return pl.pallas_call(
        kernel,
        out_shape=pltpu.VMEM((FOCUS // 16, TIME), F32),
        in_specs=[pl.BlockSpec(memory_space=pltpu.HBM)] * 4,
        out_specs=pl.BlockSpec(memory_space=pltpu.VMEM),
        scratch_shapes=[
            pltpu.VMEM((MICS, WIDE), BF),
            pltpu.VMEM((MICS, WIDE), BF),
            pltpu.VMEM((NB, MICS, FOCUS), jnp.int32),
            pltpu.VMEM((2, NB, MICS, HALF), I16),
            pltpu.VMEM((NB, MICS, HALF), I16),
            pltpu.VMEM((2, MICS, FOCUS), F32),
            pltpu.VMEM((2, 2, MICS, HALF), F32),
            pltpu.VMEM((2, MICS, HALF), F32),
            pltpu.VMEM((8, MICS, HALF), BF),
            pltpu.VMEM((8, MICS, HALF), BF),
            pltpu.VMEM((640, 128), F32),
            pltpu.VMEM((2 * SUB + 48, 512), BF),
            pltpu.VMEM((NB, SUB, HALF), F32),
            pltpu.VMEM((NB, RING, 128, 128), F32),
            pltpu.VMEM((2, NB, 4, 128, 128), BF),
            pltpu.VMEM((2, NB, 4, 128, 128), BF),
            dma((5,)),
            dma((NB,)), dma((NB,)),
            dma((NB,)), dma((NB,)),
            dma((2,)), dma((2,)),
            dma((2,)), dma((2,)),
            dma((2, NB, 4)), dma((2, NB, 4)),
        ],
        compiler_params=pltpu.CompilerParams(
            collective_id=0, has_side_effects=True, vmem_limit_bytes=40 * 1024 * 1024
        ),
    )(*(pltpu.with_memory_space_constraint(x, pltpu.HBM) for x in (signal, delay, fraction, weight)))


def solution(mesh):
    return jax.shard_map(
        shards,
        mesh=mesh,
        in_specs=(P("mic", "tm"), P("tm", "mic", None), P("mic", None), P("mic", None)),
        out_specs=P("mic", "tm"),
        check_vma=False,
    )
```
